256 devices in a mesh: tm: 32 (over y, z), head: 4 (over x_hi, core), dp: 2 (over x_lo).
Axes of the slice: x: 4 (x_hi: 2, x_lo: 2; x = x_hi * 2 + x_lo), y: 4, z: 8, core: 2. Of those that a mesh axis runs over, the one named last changes fastest.
Arguments:
- qkv: bfloat16 [2, 24576, 3, 1536], P('dp', ('tm', 'head')), may hold values from -6 to 6
- norm_gains: float32 [2, 128], replicated, may hold values from 0.1 to 1.9
- windows: int32 [12, 2], P('head'), may hold values from 0 to 1, as said below
- proj_weight: bfloat16 [1536, 3072], P(('head', 'dp')), may hold values from -0.15625 to 0.15625
- target: bfloat16 [2, 24576, 3072], P('dp', ('tm', 'head')), may hold values from -0.3125 to 0.3125
- stream_ids: int32 [2, 24576], P('dp', ('tm', 'head')), may hold values from 0 to 3
- ema_value: float32 [4], replicated, may hold values from 0.3 to 3
- ema_steps: int32 [4], replicated, may hold values from 1 to 299
Outputs:
- grad_qkv: bfloat16 [2, 24576, 3, 1536], P('dp', ('tm', 'head'))
- grad_proj: float32 [1536, 3072], P(('head', 'dp'))
- grad_gains: float32 [2, 128], replicated
The draws below stay inside these ranges and needn't reach their ends.
Inputs may be any that keep to these rules, and one draw needn't show every extreme that they name: `windows`: every entry is 0 or 1, and some head has 1 in both columns.
All inputs are finite; a program needn't handle non-finite values.
Results may differ from the reference program's by a relative error of at most 0.015.
The reference program's roundings to bfloat16 on the way count: a program that leaves them out, or rounds other values in their place, can miss the bound.
Values may be sent and summed in bfloat16 or wider, within the bound.
A program may use at most 192 MiB of HBM per device.

```python
import math
import jax
import jax.numpy as jnp
from jax import lax

D = 3072
HD = 128
HEADS = 12
TILE = 384
GW = 2
NS = 4
HH = 1536
TOKENS = 24576
CLIPS = 2
N_TM = 32


def draw_windows(key, part):
    key = jax.random.fold_in(key, 7)
    first_key, second_key = jax.random.split(key)
    reach = jax.random.randint(first_key, (HEADS, 2), 0, 2)
    chosen = jax.random.randint(second_key, (), 0, HEADS)
    rows_hit = jnp.arange(HEADS)[:, None] == chosen
    return jnp.where(rows_hit, 1, reach).astype(jnp.int32)


def plant(drawn, stream_key, least, high):
    dims = drawn.shape
    spot = [jax.random.randint(jax.random.fold_in(stream_key, axis), (), 0, dims[axis]) for axis in range(len(dims))]
    drawn = drawn.at[tuple(spot)].set(least)
    longest = dims.index(max(dims))
    spot[longest] = (spot[longest] + 1) % dims[longest]
    return drawn.at[tuple(spot)].set(high)


def level_of(rng, extent, cuts, low, top_value):
    def one(position, blocks):
        heights = jax.random.uniform(jax.random.fold_in(jax.random.fold_in(rng, 6), position), (blocks,), jnp.float32, low / len(cuts), top_value / len(cuts))
        return jnp.repeat(jnp.exp(heights), extent[position] // blocks).reshape((-1,) + (1,) * (len(extent) - position - 1))

    level = one(*cuts[0])
    for cut in cuts[1:]:
        level = level * one(*cut)
    return level


def normal_values(key, shape, scale, most, shards=(), kind=jnp.bfloat16):
    entries = jax.random.normal(key, shape, jnp.float32) * scale
    if len(shards) > 0:
        entries = level_of(key, shape, shards, -0.22, 0.18) * entries
    return jnp.clip(entries, min=-most, max=most).astype(kind)


def setup_inputs(seed: int = 0) -> dict:
    keys = jax.random.split(jax.random.key(seed), 9)
    qkv = normal_values(keys[0], (CLIPS, TOKENS, 3, HH), 1.0, 6.0, ((0, 2), (1, 128)))
    norm_gains = jnp.clip(1.0 + 0.18 * jax.random.normal(keys[1], (2, HD), jnp.float32), 0.1, 1.9)
    windows = draw_windows(jax.random.fold_in(keys[8], 71), 0)
    proj_weight = normal_values(keys[3], (HH, D), HH ** -0.5, 0.15625, ((0, 8),))
    target = normal_values(keys[4], (CLIPS, TOKENS, D), 0.05, 0.3125, ((0, 2), (1, 128)))
    stream_ids = plant(jax.random.randint(keys[5], (CLIPS, TOKENS), 0, NS), jax.random.fold_in(keys[5], 1), 0, NS - 1).astype(jnp.int32)
    ema_value = jnp.clip(jnp.exp(jax.random.uniform(keys[6], (NS,), jnp.float32, math.log(0.3), math.log(3.0))), 0.3, 3.0)
    ema_steps = plant(jax.random.randint(keys[7], (NS,), 1, 300), jax.random.fold_in(keys[7], 1), 1, 299).astype(jnp.int32)
    return dict(qkv=qkv, norm_gains=norm_gains, windows=windows, proj_weight=proj_weight, target=target, stream_ids=stream_ids, ema_value=ema_value, ema_steps=ema_steps)


EPSILON = 1e-06
DECAY_RATE = 0.99

def norm_forward(raw_part, gain_row):
    widened = raw_part.astype(jnp.float32)
    inverse = lax.rsqrt(lax.optimization_barrier(jnp.mean(widened * widened, axis=-1, keepdims=True)) + EPSILON)
    normed = widened * inverse
    return ((normed * gain_row).astype(jnp.bfloat16), normed, inverse)

def norm_backward(grad_normed, normed, inverse, gain_row):
    grad_unit = grad_normed * gain_row
    grad_input = inverse * (grad_unit - normed * lax.optimization_barrier(jnp.mean(grad_unit * normed, axis=-1, keepdims=True)))
    grad_gain = lax.optimization_barrier(jnp.sum((grad_normed * normed).reshape(-1, normed.shape[-1]), axis=0))
    return (grad_input, grad_gain)

def tile_allowed(reach, slab_len, slab_pos, slab_count):
    query_pos = jnp.arange(slab_len, dtype=jnp.int32)
    key_pos = jnp.arange(3 * slab_len, dtype=jnp.int32)
    offset = key_pos // slab_len - 1
    present = (slab_pos + offset >= 0) & (slab_pos + offset < slab_count)
    tile_gap = jnp.abs(query_pos[:, None] // TILE - key_pos[None, :] % slab_len // TILE)
    return present[None, :] & (jnp.abs(offset)[None, :] <= reach[0]) & (tile_gap <= reach[1])

def fold_back(wide_part):
    own_part = wide_part[:, 1]
    from_next = jnp.concatenate([wide_part[1:, 0], jnp.zeros_like(wide_part[:1, 0])], axis=0)
    from_prev = jnp.concatenate([jnp.zeros_like(wide_part[:1, 2]), wide_part[:-1, 2]], axis=0)
    return own_part + from_next + from_prev

def reference(qkv, norm_gains, windows, proj_weight, target, stream_ids, ema_value, ema_steps):
    slab_len = TILE * GW
    score_scale = HD ** (-0.5)
    pieces = qkv.reshape(CLIPS, N_TM, slab_len, 3, HEADS, HD)
    queries, query_unit, query_inv = norm_forward(pieces[:, :, :, 0], norm_gains[0])
    keys_n, key_unit, key_inv = norm_forward(pieces[:, :, :, 1], norm_gains[1])
    values = pieces[:, :, :, 2]
    pad_spec = ((0, 0), (1, 1), (0, 0), (0, 0), (0, 0))
    keys_pad = jnp.pad(keys_n, pad_spec)
    values_pad = jnp.pad(values, pad_spec)
    positions = jnp.arange(N_TM, dtype=jnp.int32)
    head_allowed = jax.vmap(tile_allowed, in_axes=(0, None, None, None))
    corrected = ema_value / (1.0 - jnp.power(DECAY_RATE, ema_steps.astype(jnp.float32)))
    member = (stream_ids[:, :, None] == jnp.arange(NS, dtype=jnp.int32)[None, None, :]).astype(jnp.float32)
    token_weight = jnp.einsum('cts,s->ct', member, 1.0 / corrected, precision=lax.Precision.HIGHEST)
    grad_proj = jnp.zeros((HH, D), jnp.float32)
    grad_q_all = []
    grad_k_all = []
    grad_v_all = []
    for clip in range(CLIPS):
        clip_keys = keys_pad[clip]
        clip_values = values_pad[clip]

        def blocks(slab_pos):
            key_block = lax.dynamic_slice_in_dim(clip_keys, slab_pos, 3, 0).reshape(3 * slab_len, HEADS, HD)
            value_block = lax.dynamic_slice_in_dim(clip_values, slab_pos, 3, 0).reshape(3 * slab_len, HEADS, HD)
            return (key_block, value_block)

        def chances_for(query_block, key_block, slab_pos):
            scores = jnp.einsum('qhd,khd->hqk', query_block.astype(jnp.float32), key_block.astype(jnp.float32)) * score_scale
            allowed = head_allowed(windows, slab_len, slab_pos, N_TM)
            raised = jnp.where(allowed, jnp.exp(scores), 0.0)
            return (raised / lax.optimization_barrier(jnp.sum(raised, axis=-1, keepdims=True))).astype(jnp.bfloat16)

        def forward_slab(members):
            query_block, slab_pos = members
            key_block, value_block = blocks(slab_pos)
            chances = chances_for(query_block, key_block, slab_pos)
            mixed = jnp.einsum('hqk,khd->qhd', chances.astype(jnp.float32), value_block.astype(jnp.float32))
            return mixed.astype(jnp.bfloat16)
        attended = lax.map(forward_slab, (queries[clip], positions))
        attn_rows = attended.reshape(TOKENS, HH)
        outputs = jnp.dot(attn_rows, proj_weight, preferred_element_type=jnp.float32)
        grad_out = (token_weight[clip][:, None] * (outputs - target[clip].astype(jnp.float32))).astype(jnp.bfloat16)
        grad_proj = grad_proj + jnp.dot(attn_rows.T, grad_out, preferred_element_type=jnp.float32)
        grad_attn = jnp.dot(grad_out, proj_weight.T, preferred_element_type=jnp.float32).astype(jnp.bfloat16)
        grad_heads = grad_attn.reshape(N_TM, slab_len, HEADS, HD)

        def backward_slab(members):
            query_block, grad_block, slab_pos = members
            key_block, value_block = blocks(slab_pos)
            chances = chances_for(query_block, key_block, slab_pos)
            spread = chances.astype(jnp.float32)
            grad_chances = jnp.einsum('qhd,khd->hqk', grad_block.astype(jnp.float32), value_block.astype(jnp.float32))
            diagonal = lax.optimization_barrier(jnp.sum(spread * grad_chances, axis=-1, keepdims=True))
            grad_scores = (spread * (grad_chances - diagonal) * score_scale).astype(jnp.bfloat16)
            grad_query = jnp.einsum('hqk,khd->qhd', grad_scores.astype(jnp.float32), key_block.astype(jnp.float32))
            grad_key = jnp.einsum('hqk,qhd->khd', grad_scores.astype(jnp.float32), query_block.astype(jnp.float32))
            grad_value = jnp.einsum('hqk,qhd->khd', spread, grad_block.astype(jnp.float32))
            return (grad_query, grad_key, grad_value)
        grad_query, grad_key_wide, grad_value_wide = lax.map(backward_slab, (queries[clip], grad_heads, positions))
        grad_q_all.append(grad_query)
        grad_k_all.append(fold_back(grad_key_wide.reshape(N_TM, 3, slab_len, HEADS, HD)))
        grad_v_all.append(fold_back(grad_value_wide.reshape(N_TM, 3, slab_len, HEADS, HD)))
    grad_qn = jnp.stack(grad_q_all, axis=0)
    grad_kn = jnp.stack(grad_k_all, axis=0)
    grad_values = jnp.stack(grad_v_all, axis=0)
    grad_q_in, gain_query = norm_backward(grad_qn, query_unit, query_inv, norm_gains[0])
    grad_k_in, gain_key = norm_backward(grad_kn, key_unit, key_inv, norm_gains[1])
    grad_gains = jnp.stack([gain_query, gain_key], axis=0)
    grad_qkv = jnp.stack([grad_q_in, grad_k_in, grad_values], axis=3).reshape(CLIPS, TOKENS, 3, HH).astype(jnp.bfloat16)
    return (grad_qkv, grad_proj, grad_gains)
```

```python
import math

import jax
import jax.numpy as jnp
from jax import lax
from jax.experimental import pallas as pl
from jax.experimental.pallas import tpu as pltpu
from jax.sharding import PartitionSpec as P

TILE = 384
EPSILON = 1e-06
LOG2_DECAY = math.log2(0.99)
HD = 128
NH = 3
GROUPS = 4
TOK = 192
SLAB = 768
D = 3072
DC = 768
NZ = 8
NY = 4
SCORE_SCALE = HD ** (-0.5)
LOG2E = 1.4426950408889634
BF = jnp.bfloat16
F32 = jnp.float32
MESH = pl.DeviceIdType.MESH


def dot(a, b, da, db):
    return lax.dot_general(a, b, (((da,), (db,)), ((), ())), preferred_element_type=F32)


def unit_of(raw):
    inverse = lax.rsqrt(jnp.mean(raw * raw, axis=-1, keepdims=True) + EPSILON)
    return raw * inverse, inverse


class Links:
    def __init__(self, send, recv, local):
        self.send, self.recv, self.local = send, recv, local
        self.n_remote = self.n_local = 0
        self.open = []

    def put(self, src, dst, device):
        i = self.n_remote
        self.n_remote += 1
        copy = pltpu.make_async_remote_copy(
            src_ref=src,
            dst_ref=dst,
            send_sem=self.send.at[i],
            recv_sem=self.recv.at[i],
            device_id=device,
            device_id_type=MESH,
        )
        copy.start()
        self.open.append(copy)
        return copy

    def keep(self, src, dst):
        i = self.n_local
        self.n_local += 1
        copy = pltpu.make_async_copy(src, dst, self.local.at[i])
        copy.start()
        return copy

    def finish(self):
        for copy in self.open:
            copy.wait_send()


N_REMOTE = 180
N_LOCAL = 16


def arrived(copies):
    for copy in copies:
        copy.wait_recv()


def mega(
    windows, qkv, wsh, tgt, ids, ema_value, ema_steps, gains,
    grad_out, gp_out, gains_out,
    tw, xin, dx, kvq, halo, pt, inv, attg, wbuf, tbuf, twb, gout,
    gas, gar, gao, gax, gxr, gkeep,
    gp, r1, passing, gp2, rl, gp3, r4, fin,
    hsend, hgrad, dkv, dout, dsb,
    gpart, gx, gz, gy,
    send, recv, local,
):
    links = Links(send, recv, local)
    tm = lax.axis_index("tm")
    head = lax.axis_index("head")
    dp = lax.axis_index("dp")
    y, z = tm // NZ, lax.rem(tm, NZ)
    xh, core = head // 2, lax.rem(head, 2)
    line = head * 2 + dp

    def at_line(k):
        b = lax.rem(line + k, 8)
        return {"head": b // 2, "dp": lax.rem(b, 2)}

    def at_z(k):
        return {"tm": y * NZ + lax.rem(z + k, NZ)}

    def at_y(k):
        return {"tm": lax.rem(y + k, NY) * NZ + z}

    right = {"tm": lax.rem(tm + 1, 32)}
    left = {"tm": lax.rem(tm + 31, 32)}
    sib_head = xh * 2 + (1 - core)
    cross_head = (1 - xh) * 2 + core
    diag_head = (1 - xh) * 2 + (1 - core)
    sibling, cross = {"head": sib_head}, {"head": cross_head}
    peers = [cross_head, diag_head, sib_head]

    barrier = pltpu.get_barrier_semaphore()
    greet = [at_line(k) for k in range(1, 8)] + [at_z(k) for k in range(1, 8)]
    greet += [at_y(k) for k in range(1, 4)] + [right, left]
    for device in greet:
        pl.semaphore_signal(barrier, inc=1, device_id=device, device_id_type=MESH)

    def pre(h):
        for j in range(GROUPS):
            c = slice((j * NH + h) * HD, (j * NH + h + 1) * HD)
            xin[j, h, :, :HD] = (unit_of(qkv[1, :, c].astype(F32))[0] * gains[1:2]).astype(BF)
            xin[j, h, :, HD : 2 * HD] = qkv[2, :, c]
            xin[j, h, :, 2 * HD :] = (unit_of(qkv[0, :, c].astype(F32))[0] * gains[0:1]).astype(BF)

    pre(0)
    powers = jnp.exp2(ema_steps[...].astype(F32) * LOG2_DECAY)
    stream_weight = (1.0 - powers) / ema_value[...]
    token_weight = jnp.zeros((1, TOK), F32)
    for i in range(ema_value.shape[1]):
        token_weight = jnp.where(ids[...] == i, stream_weight[:, i : i + 1], token_weight)
    tw[...] = jnp.zeros((8, 256), F32)
    tw[0:1, :TOK] = token_weight
    pl.semaphore_wait(barrier, len(greet))

    my_tok = pl.ds(pl.multiple_of(head * TOK, TOK), TOK)
    my_row = pl.ds(pl.multiple_of(y * 48, 48), 48)

    def tok_of(h):
        return pl.ds(pl.multiple_of(h * TOK, TOK), TOK)

    def send_heads(h):
        out = [links.put(xin.at[p, h], kvq.at[h, my_tok], {"head": p}) for p in peers]
        own = links.keep(xin.at[head, h], kvq.at[h, my_tok])
        return out, own

    def send_halo(h):
        src = kvq.at[h, :, pl.ds(0, 2 * HD)]
        return [links.put(src, halo.at[0, h], right), links.put(src, halo.at[1, h], left)]

    wx = []
    for k in range(1, 8):
        b = lax.rem(line + k, 8)
        cols = pl.ds(pl.multiple_of((b // 2) * DC, DC), DC)
        wx.append(links.put(wsh.at[my_row, cols], wbuf.at[line, my_row], at_line(k)))
    wown = links.keep(
        wsh.at[my_row, pl.ds(pl.multiple_of(head * DC, DC), DC)], wbuf.at[line, my_row]
    )
    x0 = send_heads(0)
    pre(1)
    pre(2)

    ahead = jnp.where(z < NZ // 2, NY - 1, 1)
    back = NY - ahead

    def row_of(k):
        return pl.ds(pl.multiple_of(lax.rem(y + k, NY) * 48, 48), 48)

    def share_w(k, to):
        rows = row_of(k)
        return links.put(wbuf.at[:, rows], wbuf.at[:, rows], at_y(to))

    arrived(wx)
    wown.wait()
    wy = [share_w(0, ahead), share_w(0, back)]
    arrived(x0[0])
    x0[1].wait()
    z0 = send_halo(0)
    x1 = send_heads(1)

    def kv(h, t):
        return kvq.at[h] if t == 1 else halo.at[t // 2, h]

    scale2 = SCORE_SCALE * LOG2E
    query_tile = lax.broadcasted_iota(jnp.int32, (1, SLAB), 1) // TILE

    def reach(h, t):
        if t == 1:
            return jnp.float32(1.0)
        present = tm > 0 if t == 0 else tm < 31
        return jnp.where(present, windows[h, 0].astype(F32), 0.0)

    def scores(h, t):
        ref = kv(h, t)
        q = kvq[h, :, 2 * HD :]
        along, across = reach(h, t), windows[h, 1].astype(F32)

        @pl.loop(0, 2)
        def _(b):
            k = ref[pl.ds(pl.multiple_of(b * TILE, TILE), TILE), :HD]
            s = dot(k, q, 1, 1)
            allowed = along * jnp.where(query_tile == b, 1.0, across)
            p = jnp.exp2(s * scale2 + (allowed - 1.0) * 1e30)
            pt[h, pl.ds(pl.multiple_of((t * 2 + b) * TILE, TILE), TILE), :] = p.astype(BF)

    ones_t = jnp.ones((HD, SLAB), BF)

    def attend(h):
        total = None
        for t in (1, 0, 2):
            vt = jnp.transpose(kv(h, t)[:, HD : 2 * HD])
            part = dot(jnp.concatenate([vt, ones_t], axis=0), pt[h, t * SLAB : (t + 1) * SLAB, :], 1, 0)
            total = part if total is None else total + part
        inverse = 1.0 / total[HD:]
        inv[h] = jnp.transpose(inverse)
        att = jnp.transpose(total[:HD] * inverse).astype(BF)
        attg[:, pl.ds(pl.multiple_of(head * TILE + h * HD, HD), HD)] = att

    scores(0, 1)
    arrived(x1[0])
    x1[1].wait()
    arrived(wy[:1])
    wy[:1] = [share_w(back, ahead)]
    z1 = send_halo(1)
    x2 = send_heads(2)
    scores(1, 1)
    arrived(x2[0])
    x2[1].wait()
    z2 = send_halo(2)
    tx = []
    for p in peers:
        cols = pl.ds(pl.multiple_of(p * DC, DC), DC)
        tx.append(links.put(tgt.at[:, cols], tbuf.at[head], {"head": p}))
        tx.append(links.put(tw, twb.at[head], {"head": p}))
    town = links.keep(tgt.at[:, pl.ds(pl.multiple_of(head * DC, DC), DC)], tbuf.at[head])
    twown = links.keep(tw, twb.at[head])
    scores(2, 1)

    def att_cols(g, h):
        return pl.ds(pl.multiple_of(g * TILE + h * HD, HD), HD)

    att_in, att_fwd = [], []

    def forward(h):
        arrived([att_in[h][0]])
        cols = att_cols(cross_head, h)
        att_fwd.append(links.put(attg.at[:, cols], attg.at[:, cols], sibling))

    for h, zh in enumerate((z0, z1, z2)):
        arrived(zh)
        scores(h, 0)
        scores(h, 2)
        attend(h)
        cols = att_cols(head, h)
        mine = attg.at[:, cols]
        att_in.append([links.put(mine, mine, cross), links.put(mine, mine, sibling)])
        if h > 0:
            forward(h - 1)
    forward(2)
    arrived(wy)
    arrived([c[1] for c in att_in])
    arrived(att_fwd)

    arrived(tx)
    town.wait()
    twown.wait()

    @pl.loop(0, GROUPS)
    def _(i):
        rows = pl.ds(pl.multiple_of(i * TOK, TOK), TOK)
        w = wbuf[...].reshape(GROUPS * TILE, DC)
        out = dot(attg[rows, :], w, 1, 0)
        col = jnp.transpose(jnp.broadcast_to(twb[i, 0:1, :], (HD, 256)))[:TOK, 0:1]
        gout[rows, :] = (col * (out - tbuf[i].astype(F32))).astype(BF)

    def w_rows(group, h):
        w = wbuf[pl.ds(group * 2, 2)].reshape(TILE, DC)
        return w[h * HD : (h + 1) * HD]

    sib_in = []
    for h in range(NH):
        w = jnp.concatenate([w_rows(sib_head, h), w_rows(diag_head, h)], axis=0)
        gas[h] = dot(gout[...], w, 1, 1).astype(BF)
        sib_in.append(links.put(gas.at[h], gar.at[h], sibling))
    for h in range(NH):
        w = jnp.concatenate([w_rows(head, h), w_rows(cross_head, h)], axis=0)
        gao[h] = dot(gout[...], w, 1, 1)
    cross_in = []
    for h in range(NH):
        arrived([sib_in[h]])
        total = gao[h] + gar[h].astype(F32)
        gkeep[h] = total[:, :HD]
        gax[h] = total[:, HD:].astype(BF)
        cross_in.append(links.put(gax.at[h], gxr.at[h], cross))

    @pl.loop(0, GROUPS)
    def _(g):
        a = attg[:, pl.ds(pl.multiple_of(g * TILE, TILE), TILE)]
        part = dot(a, gout[...], 0, 0).astype(BF)
        gp[2 * g] = part[:TOK]
        gp[2 * g + 1] = part[TOK:]

    ry_far = links.put(gp.at[:, row_of(2)], r1.at[0], at_y(ahead))
    ry_back = links.put(gp.at[:, row_of(back)], r1.at[1], at_y(back))

    lane = lax.broadcasted_iota(jnp.int32, (SLAB, HD), 1)

    def backward(h):
        arrived([cross_in[h]])
        g = (gkeep[h] + gxr[h].astype(F32)).astype(BF).astype(F32)
        g2 = (g * inv[h]).astype(BF)
        att = attg[:, att_cols(head, h)].astype(F32)
        diagonal = jnp.sum(g2.astype(F32) * att, axis=1, keepdims=True)
        high = diagonal.astype(BF).astype(F32)
        low = diagonal - high
        extra = jnp.where(lane == 0, -high, jnp.where(lane == 1, -low, 0.0)).astype(BF)
        gext = jnp.concatenate([g2, extra], axis=1)
        q = kvq[h, :, 2 * HD :]
        sent = []
        dq = None
        for t in (0, 2, 1):
            ref = kv(h, t)
            for b in range(2):
                rows = pl.ds(b * TILE, TILE)
                v = jnp.concatenate([ref[rows, HD : 2 * HD], jnp.ones((TILE, HD), BF)], axis=1)
                d = dot(v, gext, 1, 1)
                p = pt[h, (t * 2 + b) * TILE : (t * 2 + b + 1) * TILE, :]
                ds = (p.astype(F32) * d).astype(BF)
                dsb[rows, :] = ds
                dv = dot(p, g2, 1, 0)
                dk = dot(ds, q, 1, 0) * SCORE_SCALE
                if t == 1:
                    dkv[h, rows, :HD] = dk
                    dkv[h, rows, HD:] = dv
                else:
                    hsend[t // 2, h, rows, :HD] = dk.astype(BF)
                    hsend[t // 2, h, rows, HD:] = dv.astype(BF)
            if t == 0:
                sent.append(links.put(hsend.at[0, h], hgrad.at[1, h], left))
            if t == 2:
                sent.append(links.put(hsend.at[1, h], hgrad.at[0, h], right))
            kt = jnp.transpose(ref[:, :HD])
            part = dot(kt, dsb[...], 1, 0)
            dq = part if dq is None else dq + part
        dq = jnp.transpose(dq) * SCORE_SCALE
        dout[h, :, 2 * HD :] = dq.astype(BF)
        gain = jnp.sum(dq * q.astype(F32), axis=0, keepdims=True)
        q_cols = pl.ds(2 * HD, HD)
        back = [
            links.put(dout.at[h, tok_of(p), q_cols], dx.at[head, h, :, q_cols], {"head": p})
            for p in peers
        ]
        return sent, gain, back

    sent0, gq0, back0 = backward(0)
    arrived([ry_far])
    passing[...] = (gp[:, row_of(ahead)].astype(F32) + r1[0].astype(F32)).astype(BF)
    ry_ahead = links.put(passing, r1.at[2], at_y(ahead))
    sent1, gq1, back1 = backward(1)
    sent2, gq2, back2 = backward(2)

    def chunk(zz):
        return gp3.at[zz // 2, :, pl.ds(pl.multiple_of(lax.rem(zz, 2) * TILE, TILE), TILE)]

    def fold(h, sent):
        arrived(sent)
        total = dkv[h] + hgrad[0, h].astype(F32) + hgrad[1, h].astype(F32)
        dout[h, :, : 2 * HD] = total.astype(BF)
        gain = jnp.sum(total[:, :HD] * kvq[h, :, :HD].astype(F32), axis=0, keepdims=True)
        kv_cols = pl.ds(0, 2 * HD)
        back = [
            links.put(dout.at[h, tok_of(p), kv_cols], dx.at[head, h, :, kv_cols], {"head": p})
            for p in peers
        ]
        own = links.keep(dout.at[h, my_tok], dx.at[head, h])
        return gain, back, own

    def post(h):
        cols = []
        for j in range(GROUPS):
            c = slice((j * NH + h) * HD, (j * NH + h + 1) * HD)
            for i, o in ((0, 2), (1, 0)):
                unit, inverse = unit_of(qkv[i, :, c].astype(F32))
                e = dx[j, h, :, o * HD : (o + 1) * HD].astype(F32) * gains[i : i + 1]
                mean = jnp.mean(e * unit, axis=-1, keepdims=True)
                grad_out[i, :, c] = (inverse * (e - unit * mean)).astype(BF)
            grad_out[2, :, c] = dx[j, h, :, HD : 2 * HD]

    gk0, fold0, own0 = fold(0, sent0)
    arrived([ry_back, ry_ahead])
    gp2[...] = (gp[:, my_row].astype(F32) + r1[1].astype(F32) + r1[2].astype(F32)).astype(BF)
    rline = [
        links.put(gp2.at[lax.rem(line + k, 8)], rl.at[line], at_line(k)) for k in range(1, 8)
    ]
    rown = links.keep(gp2.at[line], rl.at[line])
    gk1, fold1, own1 = fold(1, sent1)
    gk2, fold2, own2 = fold(2, sent2)
    arrived(rline)
    rown.wait()
    for j in range(GROUPS):
        gp3[j] = (rl[2 * j].astype(F32) + rl[2 * j + 1].astype(F32)).astype(BF)
    rz = [links.put(chunk(lax.rem(z + k, NZ)), r4.at[k - 1], at_z(k)) for k in range(1, 8)]

    part = jnp.concatenate(
        [gq0 + gq1 + gq2, gk0 + gk1 + gk2, jnp.zeros((6, HD), F32)], axis=0
    )
    gpart[0] = part
    gains_x = [links.put(gpart.at[0], gx.at[k - 1], at_line(k)) for k in range(1, 8)]
    arrived(back0)
    arrived(fold0)
    own0.wait()
    post(0)
    arrived(gains_x)
    for k in range(7):
        part = part + gx[k]
    gpart[1] = part
    gains_z = [links.put(gpart.at[1], gz.at[k - 1], at_z(k)) for k in range(1, 8)]

    arrived(rz)
    total = chunk(z)[...].astype(F32)
    for k in range(7):
        total = total + r4[k].astype(F32)
    fin[...] = total.astype(BF)

    def place(zz):
        cols = pl.ds(pl.multiple_of(zz * TILE, TILE), TILE)
        return gp_out.at[my_row, cols]

    az = [links.put(fin, place(z), at_z(k)) for k in range(1, 8)]
    ay = [links.put(fin, place(z), at_y(k)) for k in range(1, 4)]
    azown = links.keep(fin, place(z))
    arrived(gains_z)
    for k in range(7):
        part = part + gz[k]
    gpart[2] = part
    gains_y = [links.put(gpart.at[2], gy.at[k - 1], at_y(k)) for k in range(1, 4)]
    arrived(back1)
    arrived(fold1)
    own1.wait()
    post(1)
    for i in (0, 6, 1, 5, 2, 4, 3):
        arrived([az[i]])
        got = place(lax.rem(z + NZ - 1 - i, NZ))
        ay += [links.put(got, got, at_y(k)) for k in range(1, 4)]
    arrived(gains_y)
    for k in range(3):
        part = part + gy[k]
    gains_out[...] = part[:2] / gains[...]
    arrived(back2)
    arrived(fold2)
    own2.wait()
    post(2)
    azown.wait()
    arrived(ay)
    links.finish()


def run_mega(*operands):
    any_spec = pl.BlockSpec(memory_space=pl.ANY)
    vmem = pl.BlockSpec(memory_space=pltpu.VMEM)
    v = pltpu.VMEM
    scratch = [
        v((8, 256), F32),
        v((GROUPS, NH, TOK, 3 * HD), BF),
        v((GROUPS, NH, TOK, 3 * HD), BF),
        v((NH, SLAB, 3 * HD), BF),
        v((2, NH, SLAB, 2 * HD), BF),
        v((NH, 3 * SLAB, SLAB), BF),
        v((NH, SLAB, HD), F32),
        v((SLAB, GROUPS * TILE), BF),
        v((8, TOK, DC), BF),
        v((GROUPS, TOK, DC), BF),
        v((GROUPS, 8, 256), F32),
        v((SLAB, DC), BF),
        v((NH, SLAB, 2 * HD), BF),
        v((NH, SLAB, 2 * HD), BF),
        v((NH, SLAB, 2 * HD), F32),
        v((NH, SLAB, HD), BF),
        v((NH, SLAB, HD), BF),
        v((NH, SLAB, HD), F32),
        v((8, TOK, DC), BF),
        v((3, 8, 48, DC), BF),
        v((8, 48, DC), BF),
        v((8, 48, DC), BF),
        v((8, 48, DC), BF),
        v((GROUPS, 48, DC), BF),
        v((7, 48, TILE), BF),
        v((48, TILE), BF),
        v((2, NH, SLAB, 2 * HD), BF),
        v((2, NH, SLAB, 2 * HD), BF),
        v((NH, SLAB, 2 * HD), F32),
        v((NH, SLAB, 3 * HD), BF),
        v((SLAB, SLAB), BF),
        v((3, 8, HD), F32),
        v((7, 8, HD), F32),
        v((7, 8, HD), F32),
        v((3, 8, HD), F32),
        pltpu.SemaphoreType.DMA((N_REMOTE,)),
        pltpu.SemaphoreType.DMA((N_REMOTE,)),
        pltpu.SemaphoreType.DMA((N_LOCAL,)),
    ]
    return pl.pallas_call(
        mega,
        out_shape=(
            jax.ShapeDtypeStruct((3, TOK, GROUPS * TILE), BF),
            jax.ShapeDtypeStruct((TOK, D), BF),
            jax.ShapeDtypeStruct((2, HD), F32),
        ),
        in_specs=[pl.BlockSpec(memory_space=pltpu.SMEM), vmem, any_spec, any_spec] + [vmem] * 4,
        out_specs=(vmem, vmem, vmem),
        scratch_shapes=scratch,
        compiler_params=pltpu.CompilerParams(
            collective_id=1, has_side_effects=True, vmem_limit_bytes=62 * 2**20
        ),
        name="mega",
    )(*operands)


def per_device(qkv, norm_gains, windows, proj_weight, target, stream_ids, ema_value, ema_steps):
    grad_qkv, gp, grad_gains = run_mega(
        windows,
        qkv[0].transpose(1, 0, 2),
        proj_weight,
        target[0],
        stream_ids,
        ema_value[None],
        ema_steps[None],
        norm_gains,
    )
    return (grad_qkv.transpose(1, 0, 2)[None], gp.astype(F32), grad_gains)


def solution(mesh):
    return jax.shard_map(
        per_device,
        mesh=mesh,
        in_specs=(
            P("dp", ("tm", "head"), None, None),
            P(),
            P("head", None),
            P(("head", "dp"), None),
            P("dp", ("tm", "head"), None),
            P("dp", ("tm", "head")),
            P(),
            P(),
        ),
        out_specs=(P("dp", ("tm", "head"), None, None), P(("head", "dp"), None), P()),
        check_vma=False,
    )
```

```python
import math

import jax
import jax.numpy as jnp
from jax import lax
from jax.experimental import pallas as pl
from jax.experimental.pallas import tpu as pltpu
from jax.sharding import PartitionSpec as P

TILE = 384
EPSILON = 1e-06
LOG2_DECAY = math.log2(0.99)
HD = 128
NH = 3
GROUPS = 4
TOK = 192
SLAB = 768
D = 3072
DC = 768
NZ = 8
NY = 4
SCORE_SCALE = HD ** (-0.5)
LOG2E = 1.4426950408889634
BF = jnp.bfloat16
F32 = jnp.float32
MESH = pl.DeviceIdType.MESH


def dot(a, b, da, db):
    return lax.dot_general(a, b, (((da,), (db,)), ((), ())), preferred_element_type=F32)


def unit_of(raw):
    inverse = lax.rsqrt(jnp.mean(raw * raw, axis=-1, keepdims=True) + EPSILON)
    return raw * inverse, inverse


class Links:
    def __init__(self, send, recv, local):
        self.send, self.recv, self.local = send, recv, local
        self.n_remote = self.n_local = 0
        self.open = []

    def put(self, src, dst, device):
        i = self.n_remote
        self.n_remote += 1
        copy = pltpu.make_async_remote_copy(
            src_ref=src,
            dst_ref=dst,
            send_sem=self.send.at[i],
            recv_sem=self.recv.at[i],
            device_id=device,
            device_id_type=MESH,
        )
        copy.start()
        self.open.append(copy)
        return copy

    def keep(self, src, dst):
        i = self.n_local
        self.n_local += 1
        copy = pltpu.make_async_copy(src, dst, self.local.at[i])
        copy.start()
        return copy

    def finish(self):
        for copy in self.open:
            copy.wait_send()


N_REMOTE = 180
N_LOCAL = 16


def arrived(copies):
    for copy in copies:
        copy.wait_recv()


def mega(
    windows, qkv, wsh, tgt, ids, ema_value, ema_steps, gains,
    grad_out, gp_out, gains_out,
    tw, xin, dx, kvq, halo, pt, inv, attg, wbuf, tbuf, twb, gout,
    gas, gar, gao, gax, gxr, gkeep,
    gp, r1, passing, gp2, rl, gp3, r4, fin,
    hsend, hgrad, dkv, dout, dsb,
    gpart, gx, gz, gy,
    send, recv, local,
):
    links = Links(send, recv, local)
    tm = lax.axis_index("tm")
    head = lax.axis_index("head")
    dp = lax.axis_index("dp")
    y, z = tm // NZ, lax.rem(tm, NZ)
    xh, core = head // 2, lax.rem(head, 2)
    line = head * 2 + dp

    def at_line(k):
        b = lax.rem(line + k, 8)
        return {"head": b // 2, "dp": lax.rem(b, 2)}

    def at_z(k):
        return {"tm": y * NZ + lax.rem(z + k, NZ)}

    def at_y(k):
        return {"tm": lax.rem(y + k, NY) * NZ + z}

    right = {"tm": lax.rem(tm + 1, 32)}
    left = {"tm": lax.rem(tm + 31, 32)}
    sib_head = xh * 2 + (1 - core)
    cross_head = (1 - xh) * 2 + core
    diag_head = (1 - xh) * 2 + (1 - core)
    sibling, cross = {"head": sib_head}, {"head": cross_head}
    peers = [cross_head, diag_head, sib_head]

    barrier = pltpu.get_barrier_semaphore()
    greet = [at_line(k) for k in range(1, 8)] + [at_z(k) for k in range(1, 8)]
    greet += [at_y(k) for k in range(1, 4)] + [right, left]
    for device in greet:
        pl.semaphore_signal(barrier, inc=1, device_id=device, device_id_type=MESH)

    def pre(h):
        for j in range(GROUPS):
            c = slice((j * NH + h) * HD, (j * NH + h + 1) * HD)
            xin[j, h, :, :HD] = (unit_of(qkv[1, :, c].astype(F32))[0] * gains[1:2]).astype(BF)
            xin[j, h, :, HD : 2 * HD] = qkv[2, :, c]
            xin[j, h, :, 2 * HD :] = (unit_of(qkv[0, :, c].astype(F32))[0] * gains[0:1]).astype(BF)

    pre(0)
    powers = jnp.exp2(ema_steps[...].astype(F32) * LOG2_DECAY)
    stream_weight = (1.0 - powers) / ema_value[...]
    token_weight = jnp.zeros((1, TOK), F32)
    for i in range(ema_value.shape[1]):
        token_weight = jnp.where(ids[...] == i, stream_weight[:, i : i + 1], token_weight)
    tw[...] = jnp.zeros((8, 256), F32)
    tw[0:1, :TOK] = token_weight
    pl.semaphore_wait(barrier, len(greet))

    my_tok = pl.ds(pl.multiple_of(head * TOK, TOK), TOK)
    my_row = pl.ds(pl.multiple_of(y * 48, 48), 48)

    def tok_of(h):
        return pl.ds(pl.multiple_of(h * TOK, TOK), TOK)

    def send_heads(h):
        out = [links.put(xin.at[p, h], kvq.at[h, my_tok], {"head": p}) for p in peers]
        own = links.keep(xin.at[head, h], kvq.at[h, my_tok])
        return out, own

    def send_halo(h):
        src = kvq.at[h, :, pl.ds(0, 2 * HD)]
        return [links.put(src, halo.at[0, h], right), links.put(src, halo.at[1, h], left)]

    half = lax.rem(z, 2) * TILE
    my_half = pl.ds(pl.multiple_of(half, TILE), TILE)

    def w_cols(h):
        return pl.ds(pl.multiple_of(h * DC + half, TILE), TILE)

    wx = []
    for k in range(1, 8):
        b = lax.rem(line + k, 8)
        src = wsh.at[my_row, w_cols(b // 2)]
        wx.append(links.put(src, wbuf.at[line, my_row, my_half], at_line(k)))
    wown = links.keep(wsh.at[my_row, w_cols(head)], wbuf.at[line, my_row, my_half])
    x0 = send_heads(0)
    pre(1)
    pre(2)

    ahead = jnp.where(z < NZ // 2, NY - 1, 1)
    back = NY - ahead

    def row_of(k):
        return pl.ds(pl.multiple_of(lax.rem(y + k, NY) * 48, 48), 48)

    def share_w(k, to):
        rows = row_of(k)
        return links.put(wbuf.at[:, rows], wbuf.at[:, rows], at_y(to))

    arrived(wx)
    wown.wait()
    mine = wbuf.at[:, my_row, my_half]
    wz = links.put(mine, mine, {"tm": tm + 1 - 2 * lax.rem(z, 2)})
    x1 = send_heads(1)
    arrived(x0[0])
    x0[1].wait()
    z0 = send_halo(0)
    x2 = send_heads(2)
    arrived([wz])
    wy = [share_w(0, ahead), share_w(0, back)]

    def kv(h, t):
        return kvq.at[h] if t == 1 else halo.at[t // 2, h]

    scale2 = SCORE_SCALE * LOG2E
    query_tile = lax.broadcasted_iota(jnp.int32, (1, SLAB), 1) // TILE

    def reach(h, t):
        if t == 1:
            return jnp.float32(1.0)
        present = tm > 0 if t == 0 else tm < 31
        return jnp.where(present, windows[0, h].astype(F32), 0.0)

    def scores(h, t):
        ref = kv(h, t)
        q = kvq[h, :, 2 * HD :]
        along, across = reach(h, t), windows[1, h].astype(F32)

        @pl.loop(0, 2)
        def _(b):
            k = ref[pl.ds(pl.multiple_of(b * TILE, TILE), TILE), :HD]
            s = dot(k, q, 1, 1)
            allowed = along * jnp.where(query_tile == b, 1.0, across)
            p = jnp.exp2(s * scale2 + (allowed - 1.0) * 1e30)
            pt[h, pl.ds(pl.multiple_of((t * 2 + b) * TILE, TILE), TILE), :] = p.astype(BF)

    ones_t = jnp.ones((HD, SLAB), BF)

    def attend(h):
        total = None
        for t in (1, 0, 2):
            vt = jnp.transpose(kv(h, t)[:, HD : 2 * HD])
            part = dot(jnp.concatenate([vt, ones_t], axis=0), pt[h, t * SLAB : (t + 1) * SLAB, :], 1, 0)
            total = part if total is None else total + part
        inverse = 1.0 / total[HD:]
        inv[h] = jnp.transpose(inverse)
        att = jnp.transpose(total[:HD] * inverse).astype(BF)
        attg[:, pl.ds(pl.multiple_of(head * TILE + h * HD, HD), HD)] = att

    scores(0, 1)
    arrived(x1[0])
    x1[1].wait()
    z1 = send_halo(1)
    tx = []
    for p in peers:
        cols = pl.ds(pl.multiple_of(p * DC, DC), DC)
        tx.append(links.put(tgt.at[:, cols], tbuf.at[head], {"head": p}))
        tx.append(links.put(tw, twb.at[head], {"head": p}))
    town = links.keep(tgt.at[:, pl.ds(pl.multiple_of(head * DC, DC), DC)], tbuf.at[head])
    twown = links.keep(tw, twb.at[head])
    scores(1, 1)
    arrived(x2[0])
    x2[1].wait()
    z2 = send_halo(2)
    arrived(wy[:1])
    wy[:1] = [share_w(back, ahead)]
    scores(2, 1)

    def att_cols(g, h):
        return pl.ds(pl.multiple_of(g * TILE + h * HD, HD), HD)

    att_in, att_fwd = [], []

    def forward(h):
        arrived([att_in[h][0]])
        cols = att_cols(cross_head, h)
        att_fwd.append(links.put(attg.at[:, cols], attg.at[:, cols], sibling))

    for h, zh in enumerate((z0, z1, z2)):
        arrived(zh)
        scores(h, 0)
        scores(h, 2)
        attend(h)
        cols = att_cols(head, h)
        mine = attg.at[:, cols]
        att_in.append([links.put(mine, mine, cross), links.put(mine, mine, sibling)])
        if h > 0:
            forward(h - 1)
    forward(2)
    arrived(wy)
    arrived([c[1] for c in att_in])
    arrived(att_fwd)

    arrived(tx)
    town.wait()
    twown.wait()

    @pl.loop(0, GROUPS)
    def _(i):
        rows = pl.ds(pl.multiple_of(i * TOK, TOK), TOK)
        w = wbuf[...].reshape(GROUPS * TILE, DC)
        out = dot(attg[rows, :], w, 1, 0)
        col = jnp.transpose(jnp.broadcast_to(twb[i, 0:1, :], (HD, 256)))[:TOK, 0:1]
        gout[rows, :] = (col * (out - tbuf[i].astype(F32))).astype(BF)

    @pl.loop(0, GROUPS)
    def _(g):
        a = attg[:, pl.ds(pl.multiple_of(g * TILE, TILE), TILE)]
        part = dot(a, gout[...], 0, 0).astype(BF)
        gp[2 * g] = part[:TOK]
        gp[2 * g + 1] = part[TOK:]

    ry_far = links.put(gp.at[:, row_of(2)], r1.at[0], at_y(ahead))
    ry_back = links.put(gp.at[:, row_of(back)], r1.at[1], at_y(back))

    def w_rows(group, h):
        w = wbuf[pl.ds(group * 2, 2)].reshape(TILE, DC)
        return w[h * HD : (h + 1) * HD]

    sib_in = []
    for h in range(NH):
        w = jnp.concatenate([w_rows(sib_head, h), w_rows(diag_head, h)], axis=0)
        gas[h] = dot(gout[...], w, 1, 1).astype(BF)
        sib_in.append(links.put(gas.at[h], gar.at[h], sibling))
    for h in range(NH):
        w = jnp.concatenate([w_rows(head, h), w_rows(cross_head, h)], axis=0)
        gao[h] = dot(gout[...], w, 1, 1)
    cross_in = []
    for h in range(NH):
        arrived([sib_in[h]])
        total = gao[h] + gar[h].astype(F32)
        gkeep[h] = total[:, :HD]
        gax[h] = total[:, HD:].astype(BF)
        cross_in.append(links.put(gax.at[h], gxr.at[h], cross))

    lane = lax.broadcasted_iota(jnp.int32, (SLAB, HD), 1)

    def backward(h):
        arrived([cross_in[h]])
        g = (gkeep[h] + gxr[h].astype(F32)).astype(BF).astype(F32)
        g2 = (g * inv[h]).astype(BF)
        att = attg[:, att_cols(head, h)].astype(F32)
        diagonal = jnp.sum(g2.astype(F32) * att, axis=1, keepdims=True)
        high = diagonal.astype(BF).astype(F32)
        low = diagonal - high
        extra = jnp.where(lane == 0, -high, jnp.where(lane == 1, -low, 0.0)).astype(BF)
        gext = jnp.concatenate([g2, extra], axis=1)
        q = kvq[h, :, 2 * HD :]
        sent = []
        dq = None
        for t in (0, 2, 1):
            ref = kv(h, t)
            for b in range(2):
                rows = pl.ds(b * TILE, TILE)
                v = jnp.concatenate([ref[rows, HD : 2 * HD], jnp.ones((TILE, HD), BF)], axis=1)
                d = dot(v, gext, 1, 1)
                p = pt[h, (t * 2 + b) * TILE : (t * 2 + b + 1) * TILE, :]
                ds = (p.astype(F32) * d).astype(BF)
                dsb[rows, :] = ds
                dv = dot(p, g2, 1, 0)
                dk = dot(ds, q, 1, 0) * SCORE_SCALE
                if t == 1:
                    dkv[h, rows, :HD] = dk
                    dkv[h, rows, HD:] = dv
                else:
                    hsend[t // 2, h, rows, :HD] = dk.astype(BF)
                    hsend[t // 2, h, rows, HD:] = dv.astype(BF)
            if t == 0:
                sent.append(links.put(hsend.at[0, h], hgrad.at[1, h], left))
            if t == 2:
                sent.append(links.put(hsend.at[1, h], hgrad.at[0, h], right))
            kt = jnp.transpose(ref[:, :HD])
            part = dot(kt, dsb[...], 1, 0)
            dq = part if dq is None else dq + part
        dq = jnp.transpose(dq) * SCORE_SCALE
        dout[h, :, 2 * HD :] = dq.astype(BF)
        gain = jnp.sum(dq * q.astype(F32), axis=0, keepdims=True)
        q_cols = pl.ds(2 * HD, HD)
        back = [
            links.put(dout.at[h, tok_of(p), q_cols], dx.at[head, h, :, q_cols], {"head": p})
            for p in peers
        ]
        return sent, gain, back

    sent0, gq0, back0 = backward(0)
    sent1, gq1, back1 = backward(1)
    arrived([ry_far])
    passing[...] = (gp[:, row_of(ahead)].astype(F32) + r1[0].astype(F32)).astype(BF)
    ry_ahead = links.put(passing, r1.at[2], at_y(ahead))
    sent2, gq2, back2 = backward(2)

    def chunk(zz):
        return gp3.at[zz // 2, :, pl.ds(pl.multiple_of(lax.rem(zz, 2) * TILE, TILE), TILE)]

    def fold(h, sent):
        arrived(sent)
        total = dkv[h] + hgrad[0, h].astype(F32) + hgrad[1, h].astype(F32)
        dout[h, :, : 2 * HD] = total.astype(BF)
        gain = jnp.sum(total[:, :HD] * kvq[h, :, :HD].astype(F32), axis=0, keepdims=True)
        kv_cols = pl.ds(0, 2 * HD)
        back = [
            links.put(dout.at[h, tok_of(p), kv_cols], dx.at[head, h, :, kv_cols], {"head": p})
            for p in peers
        ]
        own = links.keep(dout.at[h, my_tok], dx.at[head, h])
        return gain, back, own

    def post(h):
        cols = []
        for j in range(GROUPS):
            c = slice((j * NH + h) * HD, (j * NH + h + 1) * HD)
            for i, o in ((0, 2), (1, 0)):
                unit, inverse = unit_of(qkv[i, :, c].astype(F32))
                e = dx[j, h, :, o * HD : (o + 1) * HD].astype(F32) * gains[i : i + 1]
                mean = jnp.mean(e * unit, axis=-1, keepdims=True)
                grad_out[i, :, c] = (inverse * (e - unit * mean)).astype(BF)
            grad_out[2, :, c] = dx[j, h, :, HD : 2 * HD]

    gk0, fold0, own0 = fold(0, sent0)
    arrived([ry_back, ry_ahead])
    gp2[...] = (gp[:, my_row].astype(F32) + r1[1].astype(F32) + r1[2].astype(F32)).astype(BF)
    rline = [
        links.put(gp2.at[lax.rem(line + k, 8)], rl.at[line], at_line(k)) for k in range(1, 8)
    ]
    rown = links.keep(gp2.at[line], rl.at[line])
    gk1, fold1, own1 = fold(1, sent1)
    arrived(rline)
    rown.wait()
    for j in range(GROUPS):
        gp3[j] = (rl[2 * j].astype(F32) + rl[2 * j + 1].astype(F32)).astype(BF)
    rz = [links.put(chunk(lax.rem(z + k, NZ)), r4.at[k - 1], at_z(k)) for k in range(1, 8)]

    gk2, fold2, own2 = fold(2, sent2)

    part = jnp.concatenate(
        [gq0 + gq1 + gq2, gk0 + gk1 + gk2, jnp.zeros((6, HD), F32)], axis=0
    )
    gpart[0] = part
    gains_x = [links.put(gpart.at[0], gx.at[k - 1], at_line(k)) for k in range(1, 8)]
    arrived(back0)
    arrived(fold0)
    own0.wait()
    post(0)
    arrived(gains_x)
    for k in range(7):
        part = part + gx[k]
    gpart[1] = part
    gains_z = [links.put(gpart.at[1], gz.at[k - 1], at_z(k)) for k in range(1, 8)]

    arrived(rz)
    total = chunk(z)[...].astype(F32)
    for k in range(7):
        total = total + r4[k].astype(F32)
    fin[...] = total.astype(BF)

    def place(zz):
        cols = pl.ds(pl.multiple_of(zz * TILE, TILE), TILE)
        return gp_out.at[my_row, cols]

    az = [links.put(fin, place(z), at_z(k)) for k in range(1, 8)]
    ay = [links.put(fin, place(z), at_y(k)) for k in range(1, 4)]
    azown = links.keep(fin, place(z))
    arrived(gains_z)
    for k in range(7):
        part = part + gz[k]
    gpart[2] = part
    gains_y = [links.put(gpart.at[2], gy.at[k - 1], at_y(k)) for k in range(1, 4)]
    arrived(back1)
    arrived(fold1)
    own1.wait()
    post(1)
    for i in (0, 6, 1, 5, 2, 4, 3):
        arrived([az[i]])
        got = place(lax.rem(z + NZ - 1 - i, NZ))
        ay += [links.put(got, got, at_y(k)) for k in range(1, 4)]
    arrived(gains_y)
    for k in range(3):
        part = part + gy[k]
    gains_out[...] = part[:2] / gains[...]
    arrived(back2)
    arrived(fold2)
    own2.wait()
    post(2)
    azown.wait()
    arrived(ay)
    links.finish()


def run_mega(*operands):
    any_spec = pl.BlockSpec(memory_space=pl.ANY)
    vmem = pl.BlockSpec(memory_space=pltpu.VMEM)
    v = pltpu.VMEM
    scratch = [
        v((8, 256), F32),
        v((GROUPS, NH, TOK, 3 * HD), BF),
        v((GROUPS, NH, TOK, 3 * HD), BF),
        v((NH, SLAB, 3 * HD), BF),
        v((2, NH, SLAB, 2 * HD), BF),
        v((NH, 3 * SLAB, SLAB), BF),
        v((NH, SLAB, HD), F32),
        v((SLAB, GROUPS * TILE), BF),
        v((8, TOK, DC), BF),
        v((GROUPS, TOK, DC), BF),
        v((GROUPS, 8, 256), F32),
        v((SLAB, DC), BF),
        v((NH, SLAB, 2 * HD), BF),
        v((NH, SLAB, 2 * HD), BF),
        v((NH, SLAB, 2 * HD), F32),
        v((NH, SLAB, HD), BF),
        v((NH, SLAB, HD), BF),
        v((NH, SLAB, HD), F32),
        v((8, TOK, DC), BF),
        v((3, 8, 48, DC), BF),
        v((8, 48, DC), BF),
        v((8, 48, DC), BF),
        v((8, 48, DC), BF),
        v((GROUPS, 48, DC), BF),
        v((7, 48, TILE), BF),
        v((48, TILE), BF),
        v((2, NH, SLAB, 2 * HD), BF),
        v((2, NH, SLAB, 2 * HD), BF),
        v((NH, SLAB, 2 * HD), F32),
        v((NH, SLAB, 3 * HD), BF),
        v((SLAB, SLAB), BF),
        v((3, 8, HD), F32),
        v((7, 8, HD), F32),
        v((7, 8, HD), F32),
        v((3, 8, HD), F32),
        pltpu.SemaphoreType.DMA((N_REMOTE,)),
        pltpu.SemaphoreType.DMA((N_REMOTE,)),
        pltpu.SemaphoreType.DMA((N_LOCAL,)),
    ]
    return pl.pallas_call(
        mega,
        out_shape=(
            jax.ShapeDtypeStruct((3, TOK, GROUPS * TILE), BF),
            jax.ShapeDtypeStruct((TOK, D), BF),
            jax.ShapeDtypeStruct((2, HD), F32),
        ),
        in_specs=[pl.BlockSpec(memory_space=pltpu.SMEM), vmem, any_spec, any_spec] + [vmem] * 4,
        out_specs=(vmem, vmem, vmem),
        scratch_shapes=scratch,
        compiler_params=pltpu.CompilerParams(
            collective_id=1, has_side_effects=True, vmem_limit_bytes=62 * 2**20
        ),
        name="mega",
    )(*operands)


def per_device(qkv, norm_gains, windows, proj_weight, target, stream_ids, ema_value, ema_steps):
    grad_qkv, gp, grad_gains = run_mega(
        windows.T,
        qkv[0].transpose(1, 0, 2),
        proj_weight,
        target[0],
        stream_ids,
        ema_value[None],
        ema_steps[None],
        norm_gains,
    )
    return (grad_qkv.transpose(1, 0, 2)[None], gp.astype(F32), grad_gains)


def solution(mesh):
    return jax.shard_map(
        per_device,
        mesh=mesh,
        in_specs=(
            P("dp", ("tm", "head"), None, None),
            P(),
            P("head", None),
            P(("head", "dp"), None),
            P("dp", ("tm", "head"), None),
            P("dp", ("tm", "head")),
            P(),
            P(),
        ),
        out_specs=(P("dp", ("tm", "head"), None, None), P(("head", "dp"), None), P()),
        check_vma=False,
    )
```
